128 devices in a mesh: pipe: 8 (over z_hi, x), dp: 4 (over z_lo, core), tensor: 4 (over y).
Axes of the slice: x: 4, y: 4, z: 4 (z_hi: 2, z_lo: 2; z = z_hi * 2 + z_lo), core: 2. Of those that a mesh axis runs over, the one named last changes fastest.
Arguments:
- act_in: bfloat16 [8, 512, 4096], P('pipe', ('dp', 'tensor')), may hold values from -6 to 6
- act_first: bfloat16 [512, 4096], P(('dp', 'tensor')), may hold values from -6 to 6
- grad_in: bfloat16 [8, 512, 4096], P('pipe', ('dp', 'tensor')), may hold values from -1.5 to 1.5
- grad_last: bfloat16 [512, 4096], P(('dp', 'tensor')), may hold values from -1.5 to 1.5
- stash_local: bfloat16 [8, 2, 512, 4096], P('pipe', None, ('dp', 'tensor')), may hold values from -6 to 6
- stash_guest: bfloat16 [8, 2, 3, 512, 512], P('pipe', None, None, ('dp', 'tensor')), may hold values from -6 to 6
- plan: int32 [2, 2, 4, 4], replicated, may hold values from 0 to 7, as said below
- norm_gain: float32 [8, 4096], P('pipe'), may hold values from 0.25 to 1.75
- w_up: bfloat16 [8, 4096, 11264], P('pipe', 'dp', 'tensor'), may hold values from -0.09375 to 0.09375
- w_down: bfloat16 [8, 11264, 4096], P('pipe', 'tensor', 'dp'), may hold values from -0.0546875 to 0.0546875
Outputs:
- act_out: bfloat16 [8, 2, 512, 4096], P('pipe', None, ('dp', 'tensor'))
- grad_out: bfloat16 [8, 2, 512, 4096], P('pipe', None, ('dp', 'tensor'))
- keep_out: bfloat16 [8, 2, 512, 4096], P('pipe', None, ('dp', 'tensor'))
- guest_out: bfloat16 [8, 2, 3, 512, 512], P('pipe', None, None, ('dp', 'tensor'))
- grad_up: bfloat16 [8, 4096, 11264], P('pipe', 'dp', 'tensor')
- grad_down: bfloat16 [8, 11264, 4096], P('pipe', 'tensor', 'dp')
- grad_gain: float32 [8, 4096], P('pipe')
The draws below stay inside these ranges and needn't reach their ends.
Inputs may be any that keep to these rules, and one draw needn't show every extreme that they name: For each first index o and tick m, plan[o, m, s, 0] over s = 0 .. 3 is a permutation of 0 .. 3, with plan[o, 0, 3, 0] = 0, and plan[o, m, s, 1 ..] are 3 distinct block ids below 8.
All inputs are finite; a program needn't handle non-finite values.
Results may differ from the reference program's by a relative error of at most 0.02.
Values may be sent and summed in bfloat16 or wider, within the bound.
No kernel may reach another device: no remote copies, remote signals or barrier semaphores. Data moves between devices by JAX's collectives and lax.ppermute only.
A program may use at most 192 MiB of HBM per device.

```python
import jax
import jax.numpy as jnp
from jax import lax

D = 4096
FF = 11264
BW = 512
EVICT = 3
MICRO = 2
SECTIONS = 8
HALF = 4
ROWS = 512
BLOCKS = 8


def draw_plan(key, part):
    first_key = jax.random.fold_in(key, 11)
    second_key = jax.random.fold_in(key, 23)
    partner_scores = jax.random.randint(first_key, (2, MICRO, HALF), 0, 1 << 20) * HALF + jnp.arange(HALF, dtype=jnp.int32)
    partners = jnp.argsort(partner_scores, axis=-1, stable=True).astype(jnp.int32)
    first_tick = partners[:, 0, :]
    last_value = first_tick[:, HALF - 1]
    swapped = jnp.where(first_tick == 0, last_value[:, None], first_tick)
    swapped = swapped.at[:, HALF - 1].set(0)
    partners = partners.at[:, 0, :].set(swapped)
    block_scores = jax.random.randint(second_key, (2, MICRO, HALF, BLOCKS), 0, 1 << 20) * BLOCKS + jnp.arange(BLOCKS, dtype=jnp.int32)
    chosen = jnp.argsort(block_scores, axis=-1, stable=True)[..., :EVICT].astype(jnp.int32)
    return jnp.concatenate([partners[..., None], chosen], axis=-1)


def block_scale(stream_key, extent, shards, smallest, largest):
    loudness, own = 1.0, jax.random.fold_in(stream_key, 6)
    for axis_at, parts in shards:
        draws = jnp.exp(jax.random.uniform(jax.random.fold_in(own, axis_at), (parts,), jnp.float32, smallest / len(shards), largest / len(shards)))
        loudness = loudness * jnp.repeat(draws, extent[axis_at] // parts).reshape([-1 if axis == axis_at else 1 for axis in range(len(extent))])
    return loudness


def centred(key, dims, deviation, most, split=(), kind=jnp.bfloat16):
    values = jax.random.normal(key, dims, jnp.float32) * deviation
    if len(split) > 0:
        values = block_scale(key, dims, split, -0.22, 0.18) * values
    return jnp.clip(values, min=-most, max=most).astype(kind)


def setup_inputs(seed: int = 0) -> dict:
    splits = jax.random.split(jax.random.key(seed), 11)
    act_in = centred(splits[0], (SECTIONS, ROWS, D), 1.0, 6.0, ((0, 8), (1, 16)))
    act_first = centred(splits[1], (ROWS, D), 1.0, 6.0, ((0, 16),))
    grad_in = centred(splits[2], (SECTIONS, ROWS, D), 0.25, 1.5, ((0, 8), (1, 16)))
    grad_last = centred(splits[3], (ROWS, D), 0.25, 1.5, ((0, 16),))
    stash_local = centred(splits[4], (SECTIONS, MICRO, ROWS, D), 1.0, 6.0, ((0, 8), (2, 16)))
    stash_guest = centred(splits[5], (SECTIONS, MICRO, EVICT, ROWS, BW), 1.0, 6.0, ((0, 8), (3, 16)))
    plan = draw_plan(jax.random.fold_in(splits[10], 71), 0)
    norm_gain = jnp.clip(1.0 + 0.15 * jax.random.normal(splits[7], (SECTIONS, D), jnp.float32), 0.25, 1.75)
    w_up = centred(splits[8], (SECTIONS, D, FF), D ** -0.5, 0.09375, ((0, 8), (1, 4), (2, 4)))
    w_down = centred(splits[9], (SECTIONS, FF, D), FF ** -0.5, 0.0546875, ((0, 8), (1, 4), (2, 4)))
    return dict(act_in=act_in, act_first=act_first, grad_in=grad_in, grad_last=grad_last, stash_local=stash_local, stash_guest=stash_guest, plan=plan, norm_gain=norm_gain, w_up=w_up, w_down=w_down)


EPSILON = 1e-05

def normalize(values, norm_scale):
    wide = values.astype(jnp.float32)
    inverse_rms = lax.rsqrt(lax.optimization_barrier(jnp.mean(wide * wide, axis=-1, keepdims=True)) + EPSILON)
    return (wide, inverse_rms, wide * inverse_rms * norm_scale)

def finish_norm(wide, inverse_rms, norm_scale, d_normed, cotangent):
    scaled = d_normed * norm_scale
    d_input = cotangent.astype(jnp.float32) + inverse_rms * scaled - wide * (inverse_rms * inverse_rms * inverse_rms) * lax.optimization_barrier(jnp.mean(scaled * wide, axis=-1, keepdims=True))
    return (d_input.astype(jnp.bfloat16), lax.optimization_barrier(jnp.sum(d_normed * wide * inverse_rms, axis=0)))

def local_grads(normed_low, cotangent, up_matrix, down_matrix):
    hidden_pre = jnp.dot(normed_low, up_matrix, preferred_element_type=jnp.float32)
    sigmoid_gate = jax.nn.sigmoid(hidden_pre)
    hidden = jax.nn.silu(hidden_pre).astype(jnp.bfloat16)
    d_hidden = lax.dot_general(cotangent, down_matrix, (((1,), (1,)), ((), ())), preferred_element_type=jnp.float32)
    d_pre = (d_hidden * sigmoid_gate * (1.0 + hidden_pre * (1.0 - sigmoid_gate))).astype(jnp.bfloat16)
    grad_down_part = lax.dot_general(hidden, cotangent, (((0,), (0,)), ((), ())), preferred_element_type=jnp.float32)
    grad_up_part = lax.dot_general(normed_low, d_pre, (((0,), (0,)), ((), ())), preferred_element_type=jnp.float32)
    return (d_pre, grad_up_part, grad_down_part)

def match_blocks(block_ids, block_count):
    return block_ids[:, None] == jnp.arange(block_count, dtype=jnp.int32)[None, :]

def pull_blocks(values, block_ids, block_width):
    row_total = values.shape[0]
    blocks = values.reshape(row_total, values.shape[1] // block_width, block_width)
    return jnp.transpose(jnp.take(blocks, block_ids, axis=1), (1, 0, 2))

def clear_blocks(values, block_ids, block_width):
    row_total = values.shape[0]
    block_count = values.shape[1] // block_width
    covered = jnp.any(match_blocks(block_ids, block_count), axis=0)
    blocks = values.reshape(row_total, block_count, block_width)
    return jnp.where(covered[None, :, None], jnp.zeros((), values.dtype), blocks).reshape(values.shape)

def place_blocks(values, block_ids, fetched):
    row_total = values.shape[0]
    block_width = fetched.shape[2]
    block_count = values.shape[1] // block_width
    matched = match_blocks(block_ids, block_count)
    covered = jnp.any(matched, axis=0)
    fetched_cols = jnp.einsum('eb,erw->rbw', matched.astype(jnp.float32), fetched.astype(jnp.float32))
    blocks = values.reshape(row_total, block_count, block_width).astype(jnp.float32)
    return jnp.where(covered[None, :, None], fetched_cols, blocks).reshape(values.shape).astype(values.dtype)

def forward(values, norm_scale, up_matrix, down_matrix):
    wide, inverse_rms, normed = normalize(values, norm_scale)
    hidden = jax.nn.silu(jnp.dot(normed.astype(jnp.bfloat16), up_matrix, preferred_element_type=jnp.float32)).astype(jnp.bfloat16)
    return (wide + jnp.dot(hidden, down_matrix, preferred_element_type=jnp.float32)).astype(jnp.bfloat16)

def backward(values, cotangent, norm_scale, up_matrix, down_matrix):
    wide, inverse_rms, normed = normalize(values, norm_scale)
    d_pre, grad_up_part, grad_down_part = local_grads(normed.astype(jnp.bfloat16), cotangent, up_matrix, down_matrix)
    d_normed = lax.dot_general(d_pre, up_matrix, (((1,), (1,)), ((), ())), preferred_element_type=jnp.float32)
    d_input, gain_part = finish_norm(wide, inverse_rms, norm_scale, d_normed, cotangent)
    return (d_input, gain_part, grad_up_part, grad_down_part)

def reference(act_in, act_first, grad_in, grad_last, stash_local, stash_guest, plan, norm_gain, w_up, w_down):
    layer_in = {}
    front = {}
    for position in range(SECTIONS):
        layer_in[position, 0] = act_in[position]
        front[position, 0] = forward(act_in[position], norm_gain[position], w_up[position], w_down[position])
    for position in range(SECTIONS):
        source = act_first if position == 0 else front[position - 1, 0]
        layer_in[position, 1] = source
        front[position, 1] = forward(source, norm_gain[position], w_up[position], w_down[position])

    def stashed(position, tick):
        own = stash_local[position, tick]
        if position >= HALF:
            return own
        holder = HALF + plan[0, tick, position, 0]
        return place_blocks(own, plan[0, tick, position, 1:], stash_guest[holder, tick])
    back = {}
    for position in range(SECTIONS):
        back[position, 0] = backward(stashed(position, 0), grad_in[position], norm_gain[position], w_up[position], w_down[position])
    for position in range(SECTIONS):
        cotangent = grad_last if position == SECTIONS - 1 else back[position + 1, 0][0]
        back[position, 1] = backward(stashed(position, 1), cotangent, norm_gain[position], w_up[position], w_down[position])
    act_out = jnp.stack([jnp.stack([front[position, 0], front[position, 1]]) for position in range(SECTIONS)])
    grad_out = jnp.stack([jnp.stack([back[position, 0][0], back[position, 1][0]]) for position in range(SECTIONS)])
    grad_gain = jnp.stack([back[position, 0][1] + back[position, 1][1] for position in range(SECTIONS)])
    grad_up = jnp.stack([(back[position, 0][2] + back[position, 1][2]).astype(jnp.bfloat16) for position in range(SECTIONS)])
    grad_down = jnp.stack([(back[position, 0][3] + back[position, 1][3]).astype(jnp.bfloat16) for position in range(SECTIONS)])
    keep_rows = []
    guest_rows = []
    for position in range(SECTIONS):
        keep_ticks = []
        guest_ticks = []
        for tick in range(MICRO):
            if position < HALF:
                keep_ticks.append(clear_blocks(layer_in[position, tick], plan[1, tick, position, 1:], BW))
                guest_ticks.append(jnp.zeros((EVICT, ROWS, BW), jnp.bfloat16))
            else:
                keep_ticks.append(layer_in[position, tick])
                gathered = jnp.zeros((EVICT, ROWS, BW), jnp.float32)
                for owner in range(HALF):
                    matched = plan[1, tick, owner, 0] + HALF == position
                    blocks = pull_blocks(layer_in[owner, tick], plan[1, tick, owner, 1:], BW).astype(jnp.float32)
                    gathered = gathered + jnp.where(matched, blocks, jnp.zeros((), jnp.float32))
                guest_ticks.append(gathered.astype(jnp.bfloat16))
        keep_rows.append(jnp.stack(keep_ticks))
        guest_rows.append(jnp.stack(guest_ticks))
    keep_out = jnp.stack(keep_rows)
    guest_out = jnp.stack(guest_rows)
    return (act_out, grad_out, keep_out, guest_out, grad_up, grad_down, grad_gain)
```

```python
import jax
import jax.numpy as jnp
from jax import lax
from jax.sharding import PartitionSpec as P

MICRO = 2


EPSILON = 1e-05


def in_blocks(shard, dim, devices):
    before, after = (shard.shape[:dim], shard.shape[dim + 1 :])
    return jnp.moveaxis(shard.reshape(*before, devices, -1, *after), dim, 0)


def sum_at_owner(shard, axis, dim):
    devices = lax.axis_size(axis)
    blocks = lax.all_to_all(in_blocks(shard, dim, devices), axis, 0, 0, tiled=True)
    return jnp.sum(blocks.astype(jnp.float32), axis=0)


def laid_out(blocks, dim):
    lengths = list(blocks.shape[1:])
    lengths[dim] *= blocks.shape[0]
    return jnp.moveaxis(blocks, 0, dim).reshape(lengths)


def from_everyone(shard, axis):
    copies = jnp.broadcast_to(shard, (lax.axis_size(axis), *shard.shape))
    return lax.all_to_all(copies, axis, split_axis=0, concat_axis=0, tiled=True)


def collect(shard, axis, dim):
    return laid_out(from_everyone(shard, axis), dim)


def side_by_side(arrays, axis, dim, along):
    both = jnp.concatenate(arrays, axis=along)
    filled, at, finished = (lax.all_gather(both, axis, axis=dim, tiled=True), 0, [])
    for a in arrays:
        finished.append(lax.slice_in_dim(filled, at, at + a.shape[along], axis=along))
        at += a.shape[along]
    return tuple(finished)


def passed_along(value, axis, steps):
    count = lax.axis_size(axis)
    first, last = (max(0, -steps), min(count, count - steps))
    return lax.ppermute(value, axis, [(source, source + steps) for source in range(first, last)])


def over_copies(shard, axis):
    everything = from_everyone(shard, axis)
    return jnp.sum(everything, axis=0)


def normalize(values, norm_scale):
    wide = values.astype(jnp.float32)
    inverse_rms = lax.rsqrt(jnp.mean(wide * wide, axis=-1, keepdims=True) + EPSILON)
    return (wide, inverse_rms, wide * inverse_rms * norm_scale)


def finish_norm(wide, inverse_rms, norm_scale, d_normed, cotangent):
    scaled = d_normed * norm_scale
    d_input = (
        cotangent.astype(jnp.float32)
        + inverse_rms * scaled
        - wide
        * (inverse_rms * inverse_rms * inverse_rms)
        * jnp.mean(scaled * wide, axis=-1, keepdims=True)
    )
    return (d_input.astype(jnp.bfloat16), jnp.sum(d_normed * wide * inverse_rms, axis=0))


def match_blocks(block_ids, block_count):
    return block_ids[:, None] == jnp.arange(block_count, dtype=jnp.int32)[None, :]


def pull_blocks(values, block_ids, block_width):
    row_total = values.shape[0]
    blocks = values.reshape(row_total, values.shape[1] // block_width, block_width)
    count = block_ids.shape[0]
    picked = [
        lax.dynamic_slice_in_dim(blocks, block_ids[e], 1, axis=1)[:, 0] for e in range(count)
    ]
    return jnp.stack(picked)


def clear_blocks(values, block_ids, block_width):
    row_total = values.shape[0]
    block_count = values.shape[1] // block_width
    covered = jnp.any(match_blocks(block_ids, block_count), axis=0)
    blocks = values.reshape(row_total, block_count, block_width)
    return jnp.where(covered[None, :, None], jnp.zeros((), values.dtype), blocks).reshape(
        values.shape
    )


def place_blocks(values, block_ids, fetched):
    row_total = values.shape[0]
    block_width = fetched.shape[2]
    block_count = values.shape[1] // block_width
    matched = match_blocks(block_ids, block_count)
    covered = jnp.any(matched, axis=0)
    fetched_cols = jnp.einsum(
        "eb,erw->rbw", matched.astype(jnp.float32), fetched.astype(jnp.float32)
    )
    blocks = values.reshape(row_total, block_count, block_width).astype(jnp.float32)
    return (
        jnp.where(covered[None, :, None], fetched_cols, blocks)
        .reshape(values.shape)
        .astype(values.dtype)
    )


def settle(partial_value, row_count):
    data_count = lax.axis_size("dp")
    tensor_count = lax.axis_size("tensor")
    shaped = partial_value.reshape(data_count, tensor_count, row_count, partial_value.shape[1])
    reduced = sum_at_owner(shaped.astype(jnp.bfloat16), "tensor", 1)
    placed = lax.all_to_all(
        reduced.astype(jnp.bfloat16), "dp", split_axis=0, concat_axis=3, tiled=True
    ).astype(reduced.dtype)
    return placed.reshape(row_count, placed.shape[3])


def forward_pass(values, norm_scale, up_matrix, down_matrix):
    wide, inverse_rms, normed = normalize(values, norm_scale)
    normed_low = normed.astype(jnp.bfloat16)
    replica_rows = collect(normed_low, "tensor", 0)
    row_block = lax.all_to_all(replica_rows, "dp", split_axis=1, concat_axis=0, tiled=True)
    hidden_pre = sum_at_owner(
        jnp.dot(row_block, up_matrix, preferred_element_type=jnp.float32).astype(jnp.bfloat16),
        "dp",
        0,
    )
    hidden = jax.nn.silu(hidden_pre).astype(jnp.bfloat16)
    partial_value = jnp.dot(
        lax.all_gather(hidden, "dp", axis=0, tiled=True),
        down_matrix,
        preferred_element_type=jnp.float32,
    )
    summed = settle(partial_value, values.shape[0])
    return (wide + summed).astype(jnp.bfloat16)


def backward_pass(values, cotangent, norm_scale, up_matrix, down_matrix, grad_pair):
    wide, inverse_rms, normed = normalize(values, norm_scale)
    normed_low = normed.astype(jnp.bfloat16)
    replica_normed, replica_cotan = side_by_side((normed_low, cotangent), "tensor", 0, 1)
    normed_block, cotan_block = (
        lax.all_to_all(replica_normed, "dp", split_axis=1, concat_axis=0, tiled=True),
        lax.all_to_all(replica_cotan, "dp", split_axis=1, concat_axis=0, tiled=True),
    )
    hidden_width = up_matrix.shape[1]
    pre_part = jnp.dot(normed_block, up_matrix, preferred_element_type=jnp.float32)
    back_part = lax.dot_general(
        cotan_block, down_matrix, (((1,), (1,)), ((), ())), preferred_element_type=jnp.float32
    )
    joined = lax.psum_scatter(
        jnp.concatenate([pre_part, back_part], axis=1).astype(jnp.bfloat16),
        "dp",
        scatter_dimension=0,
        tiled=True,
    ).astype(jnp.float32)
    hidden_pre = joined[:, :hidden_width]
    d_hidden = joined[:, hidden_width:]
    sigmoid_gate = jax.nn.sigmoid(hidden_pre)
    hidden = jax.nn.silu(hidden_pre).astype(jnp.bfloat16)
    d_pre = (d_hidden * sigmoid_gate * (1.0 + hidden_pre * (1.0 - sigmoid_gate))).astype(
        jnp.bfloat16
    )
    grad_up_acc = grad_pair[0]
    grad_down_acc = grad_pair[1]
    hidden_piece = lax.all_gather(hidden, "dp", axis=0, tiled=True)
    d_pre_piece = lax.all_gather(d_pre, "dp", axis=0, tiled=True)
    grad_up_acc = grad_up_acc + lax.dot_general(
        normed_block, d_pre_piece, (((0,), (0,)), ((), ())), preferred_element_type=jnp.float32
    )
    grad_down_acc = grad_down_acc + lax.dot_general(
        hidden_piece, cotan_block, (((0,), (0,)), ((), ())), preferred_element_type=jnp.float32
    )
    normed_part = lax.dot_general(
        d_pre_piece, up_matrix, (((1,), (1,)), ((), ())), preferred_element_type=jnp.float32
    )
    normed_grad = normed_part
    grad_up_acc, grad_down_acc, normed_grad = (grad_up_acc, grad_down_acc, normed_grad)
    d_normed = settle(normed_grad, values.shape[0])
    d_input, gain_part = finish_norm(wide, inverse_rms, norm_scale, d_normed, cotangent)
    return (d_input, gain_part, (grad_up_acc, grad_down_acc))


def local(
    act_in, act_first, grad_in, grad_last, stash_local, stash_guest, plan, norm_gain, w_up, w_down
):
    section_count = lax.axis_size("pipe")
    half_sections = section_count // 2
    section_index = lax.axis_index("pipe")
    is_early = section_index < half_sections
    plan_row = jnp.minimum(section_index, half_sections - 1)
    block_width = stash_guest.shape[-1]
    norm_scale = norm_gain[0]
    up_matrix = w_up[0]
    down_matrix = w_down[0]
    section_ids = jnp.arange(section_count, dtype=jnp.int32)
    clipped_ids = jnp.minimum(section_ids, half_sections - 1)
    section_early = section_ids < half_sections
    zero_low = jnp.zeros((), jnp.bfloat16)
    old_holder = plan[0, :, :, 0] + half_sections
    sends_back = section_early[:, None] & (
        jnp.transpose(old_holder[:, clipped_ids]) == section_index
    )
    outgoing = jnp.where(sends_back[:, :, None, None, None], stash_guest[0][None], zero_low)
    source_pick = section_ids[:, None] == old_holder[:, plan_row][None, :]
    arrived = lax.all_to_all(outgoing, "pipe", split_axis=0, concat_axis=0, tiled=True)
    fetched_all = jnp.sum(jnp.where(source_pick[:, :, None, None, None], arrived, zero_low), axis=0)
    fetched_list = [fetched_all[tick] for tick in range(MICRO)]
    stash_rows = []
    for tick in range(MICRO):
        own = stash_local[0, tick]
        merged = place_blocks(own, plan[0, tick, plan_row, 1:], fetched_list[tick])
        stash_rows.append(jnp.where(is_early, merged, own))
    front_zero = forward_pass(act_in[0], norm_scale, up_matrix, down_matrix)
    passed = passed_along(front_zero, "pipe", 1)
    input_one = jnp.where(section_index == 0, act_first, passed)
    front_one = forward_pass(input_one, norm_scale, up_matrix, down_matrix)
    empty_pair = (
        jnp.zeros(up_matrix.shape, jnp.float32),
        jnp.zeros(down_matrix.shape, jnp.float32),
    )
    back_zero = backward_pass(
        stash_rows[0], grad_in[0], norm_scale, up_matrix, down_matrix, empty_pair
    )
    returned = passed_along(back_zero[0], "pipe", -1)
    cot_one = jnp.where(section_index == section_count - 1, grad_last, returned)
    back_one = backward_pass(
        stash_rows[1], cot_one, norm_scale, up_matrix, down_matrix, back_zero[2]
    )
    gain_grad = over_copies(back_zero[1] + back_one[1], ("dp", "tensor"))
    new_inputs = [act_in[0], input_one]
    new_holder = plan[1, :, :, 0] + half_sections
    pulled = jnp.stack(
        [
            pull_blocks(new_inputs[tick], plan[1, tick, plan_row, 1:], block_width)
            for tick in range(MICRO)
        ]
    )
    heading = is_early & (section_ids[:, None] == new_holder[:, plan_row][None, :])
    parcels = jnp.where(heading[:, :, None, None, None], pulled[None], zero_low)
    landed = lax.all_to_all(parcels, "pipe", split_axis=0, concat_axis=0, tiled=True)
    coming = section_early[:, None] & (jnp.transpose(new_holder[:, clipped_ids]) == section_index)
    guest_new = jnp.sum(jnp.where(coming[:, :, None, None, None], landed, zero_low), axis=0)
    kept = jnp.stack(
        [
            jnp.where(
                is_early,
                clear_blocks(new_inputs[tick], plan[1, tick, plan_row, 1:], block_width),
                new_inputs[tick],
            )
            for tick in range(MICRO)
        ]
    )
    act_out = jnp.stack([front_zero, front_one])[None]
    grad_out = jnp.stack([back_zero[0], back_one[0]])[None]
    grad_up = back_one[2][0].astype(jnp.bfloat16)[None]
    grad_down = back_one[2][1].astype(jnp.bfloat16)[None]
    return (act_out, grad_out, kept[None], guest_new[None], grad_up, grad_down, gain_grad[None])


def solution(mesh):
    placed = (
        P("pipe", ("dp", "tensor"), None),
        P(("dp", "tensor"), None),
        P("pipe", ("dp", "tensor"), None),
        P(("dp", "tensor"), None),
        P("pipe", None, ("dp", "tensor"), None),
        P("pipe", None, None, ("dp", "tensor"), None),
        P(),
        P("pipe", None),
        P("pipe", "dp", "tensor"),
        P("pipe", "tensor", "dp"),
    )
    return jax.shard_map(
        local,
        mesh=mesh,
        in_specs=placed,
        out_specs=(
            P("pipe", None, ("dp", "tensor"), None),
            P("pipe", None, ("dp", "tensor"), None),
            P("pipe", None, ("dp", "tensor"), None),
            P("pipe", None, None, ("dp", "tensor"), None),
            P("pipe", "dp", "tensor"),
            P("pipe", "tensor", "dp"),
            P("pipe", None),
        ),
        check_vma=False,
    )
```

```python
import jax
import jax.numpy as jnp
from jax import lax
from jax.sharding import PartitionSpec as P

MICRO = 2
EPSILON = 1e-05
LOW = jnp.bfloat16
WIDE = jnp.float32


def across_core(x):
    return lax.ppermute(x, "dp", [(d, d ^ 1) for d in range(4)])


def across_z(x):
    return lax.ppermute(x, "dp", [(d, d ^ 2) for d in range(4)])


def along_y(x, step):
    return lax.ppermute(x, "tensor", [(t, (t + step) % 4) for t in range(4)])


def round_x(x, step, first):
    return lax.ppermute(x, "pipe", [(first + i, first + (i + step) % 4) for i in range(4)])


def passed_along(value, steps):
    first, last = max(0, -steps), min(8, 8 - steps)
    return lax.ppermute(value, "pipe", [(s, s + steps) for s in range(first, last)])


def normalize(values, norm_scale):
    wide = values.astype(WIDE)
    inverse_rms = lax.rsqrt(jnp.mean(wide * wide, axis=-1, keepdims=True) + EPSILON)
    return wide, inverse_rms, (wide * inverse_rms * norm_scale).astype(LOW)


def finish_norm(wide, inverse_rms, norm_scale, d_normed, cotangent):
    scaled = d_normed * norm_scale
    d_input = (
        cotangent.astype(WIDE)
        + inverse_rms * scaled
        - wide
        * (inverse_rms * inverse_rms * inverse_rms)
        * jnp.mean(scaled * wide, axis=-1, keepdims=True)
    )
    return d_input.astype(LOW), jnp.sum(d_normed * wide * inverse_rms, axis=0)


def ordered(at_zero, own, other):
    return jnp.where(at_zero, own, other), jnp.where(at_zero, other, own)


class Place:
    def __init__(self):
        d = lax.axis_index("dp")
        self.z, self.core = d // 2, d % 2
        self.low_z, self.low_core = self.z == 0, self.core == 0


def gather_rows(x, place):
    rows, width = x.shape
    left, right = x[:, : width // 2], x[:, width // 2 :]
    keep = jnp.where(place.low_z, left, right)
    got = across_z(jnp.where(place.low_z, right, left))
    mine = jnp.stack(ordered(place.low_z, keep, got))
    before, after = along_y(mine, 1), along_y(mine, -1)
    far = jnp.stack([along_y(before[0], 1), along_y(after[1], -1)])
    ring = jnp.stack([mine, after, far, before])
    return jnp.concatenate([ring, across_core(ring)]).reshape(16 * rows, width // 2)


def settle(part, place):
    half, width = part.shape[0] // 2, part.shape[1]
    rows = half // 8
    got = across_core(part[half:].astype(LOW))
    summed = (part[:half] + got.astype(WIDE)).reshape(4, 2, rows, width)
    up = along_y(summed[2, 0].astype(LOW), 1).astype(WIDE)
    down = along_y(summed[2, 1].astype(LOW), -1).astype(WIDE)
    to_next = jnp.stack([summed[1, 0] + up, summed[1, 1]]).astype(LOW)
    to_last = jnp.stack([summed[3, 0], summed[3, 1] + down]).astype(LOW)
    mine = (
        summed[0] + along_y(to_next, 1).astype(WIDE) + along_y(to_last, -1).astype(WIDE)
    ).astype(LOW)
    keep = jnp.where(place.low_z, mine[0], mine[1])
    got = across_z(jnp.where(place.low_z, mine[1], mine[0]))
    return jnp.concatenate(ordered(place.low_z, keep, got), axis=1).astype(WIDE)


def summed_over_z(part):
    low = part.astype(LOW)
    return low.astype(WIDE) + across_z(low).astype(WIDE)


def whole_hidden(own, place):
    half = own.shape[0] // 2
    got = across_core(own)
    other = jnp.concatenate([got[half:], got[:half]])
    return jnp.concatenate(ordered(place.low_core, own, other), axis=1)


def my_features(x, place):
    half = x.shape[1] // 2
    return jnp.where(place.low_core, x[:, :half], x[:, half:])


def times_transposed(a, b):
    return lax.dot_general(a, b, (((1,), (1,)), ((), ())), preferred_element_type=WIDE)


def over_rows(a, b):
    return lax.dot_general(a, b, (((0,), (0,)), ((), ())), preferred_element_type=WIDE)


def match_blocks(block_ids, block_count):
    return block_ids[:, None] == jnp.arange(block_count, dtype=jnp.int32)[None, :]


def pull_blocks(values, block_ids, block_width):
    blocks = values.reshape(values.shape[0], -1, block_width)
    picked = [
        lax.dynamic_slice_in_dim(blocks, block_ids[e], 1, axis=1)[:, 0]
        for e in range(block_ids.shape[0])
    ]
    return jnp.stack(picked)


def clear_blocks(values, block_ids, block_width, active):
    blocks = values.reshape(values.shape[0], -1, block_width)
    covered = jnp.any(match_blocks(block_ids, blocks.shape[1]), axis=0) & active
    return jnp.where(covered[None, :, None], jnp.zeros((), values.dtype), blocks).reshape(
        values.shape
    )


def place_blocks(values, block_ids, fetched, active):
    block_width = fetched.shape[2]
    blocks = values.reshape(values.shape[0], -1, block_width)
    matched = match_blocks(block_ids, blocks.shape[1]) & active
    for e in range(fetched.shape[0]):
        blocks = jnp.where(matched[e][None, :, None], fetched[e][:, None, :], blocks)
    return blocks.reshape(values.shape)


def pick(options, wanted):
    total = jnp.where(wanted[0], options[0], jnp.zeros((), options[0].dtype))
    for option, want in zip(options[1:], wanted[1:]):
        total = jnp.where(want, option, total)
    return total


def guests_back(held, plan, section):
    column = section % 4
    around = [held, round_x(held, -1, 4), round_x(held, -2, 4), round_x(held, 1, 4)]
    found = []
    for tick in range(MICRO):
        holder = plan[0, tick, column, 0]
        found.append(
            pick(
                [a[tick] for a in around],
                [holder == (column + k) % 4 for k in range(4)],
            )
        )
    return lax.ppermute(jnp.stack(found), "pipe", [(4 + s, s) for s in range(4)])


def guests_out(pulled, plan_tick, section):
    column = section % 4
    landed = lax.ppermute(pulled, "pipe", [(s, 4 + s) for s in range(4)])
    around = [landed, round_x(landed, -1, 4), round_x(landed, -2, 4), round_x(landed, 1, 4)]
    late = section >= 4
    wanted = [late & (plan_tick[(column + k) % 4, 0] == column) for k in range(4)]
    return pick(around, wanted)


def over_copies(x):
    x = x + across_core(x)
    x = x + across_z(x)
    for bit in (1, 2):
        x = x + lax.ppermute(x, "tensor", [(t, t ^ bit) for t in range(4)])
    return x


def local(
    act_in, act_first, grad_in, grad_last, stash_local, stash_guest, plan, norm_gain, w_up, w_down
):
    place = Place()
    section = lax.axis_index("pipe")
    is_early = section < 4
    plan_row = jnp.minimum(section, 3)
    block_width = stash_guest.shape[-1]
    norm_scale = norm_gain[0]

    half = w_up.shape[2] // 2
    up_left, up_right = w_up[0][:, :half], w_up[0][:, half:]
    up_own = jnp.where(place.low_core, up_left, up_right)
    up_got = across_core(jnp.where(place.low_core, up_right, up_left))
    up = jnp.concatenate(ordered(place.low_core, up_own, up_got), axis=0)
    down_top, down_bottom = w_down[0][:half], w_down[0][half:]
    down_own = jnp.where(place.low_core, down_top, down_bottom)
    down_got = across_core(jnp.where(place.low_core, down_bottom, down_top))
    down = jnp.concatenate(ordered(place.low_core, down_own, down_got), axis=1)

    def forward_head(values):
        _, _, normed = normalize(values, norm_scale)
        rows = gather_rows(normed, place)
        return jnp.dot(rows, up, preferred_element_type=WIDE)

    def forward_tail(values, hidden_pre):
        hidden = jax.nn.silu(hidden_pre).astype(LOW)
        partial = jnp.dot(hidden, down, preferred_element_type=WIDE)
        return (values.astype(WIDE) + settle(partial, place)).astype(LOW)

    def backward_tail(values, inverse_rms, cotangent, hidden_pre, d_hidden):
        gate = jax.nn.sigmoid(hidden_pre)
        hidden = (hidden_pre * gate).astype(LOW)
        d_pre = (d_hidden * gate * (1.0 + hidden_pre * (1.0 - gate))).astype(LOW)
        d_normed = settle(times_transposed(d_pre, up), place)
        d_input, gain = finish_norm(
            values.astype(WIDE), inverse_rms, norm_scale, d_normed, cotangent
        )
        return d_input, gain, whole_hidden(hidden, place), whole_hidden(d_pre, place)

    guests = guests_back(stash_guest[0], plan, section)
    old = [
        place_blocks(stash_local[0, m], plan[0, m, plan_row, 1:], guests[m], is_early)
        for m in range(MICRO)
    ]
    stash_norm = [normalize(old[m], norm_scale) for m in range(MICRO)]

    cot_zero = grad_in[0]
    cot_rows_zero = gather_rows(cot_zero, place)
    d_hidden_zero = summed_over_z(times_transposed(cot_rows_zero, down))
    stash_rows = [gather_rows(stash_norm[m][2], place) for m in range(MICRO)]
    pre_zero = summed_over_z(jnp.dot(stash_rows[0], up, preferred_element_type=WIDE))

    front_pre_zero = summed_over_z(forward_head(act_in[0]))
    d_input_zero, gain_zero, hidden_zero, d_pre_zero = backward_tail(
        old[0], stash_norm[0][1], cot_zero, pre_zero, d_hidden_zero
    )
    pre_one = summed_over_z(jnp.dot(stash_rows[1], up, preferred_element_type=WIDE))
    front_zero = forward_tail(act_in[0], front_pre_zero)

    returned = passed_along(d_input_zero, -1)
    cot_one = jnp.where(section == 7, grad_last, returned)
    cot_rows_one = gather_rows(cot_one, place)
    d_hidden_one = summed_over_z(times_transposed(cot_rows_one, down))

    passed = passed_along(front_zero, 1)
    input_one = jnp.where(section == 0, act_first, passed)
    front_pre_one = summed_over_z(forward_head(input_one))

    d_input_one, gain_one, hidden_one, d_pre_one = backward_tail(
        old[1], stash_norm[1][1], cot_one, pre_one, d_hidden_one
    )
    front_one = forward_tail(input_one, front_pre_one)

    grad_up = (
        over_rows(my_features(stash_rows[0], place), d_pre_zero)
        + over_rows(my_features(stash_rows[1], place), d_pre_one)
    ).astype(LOW)
    grad_down = (
        over_rows(hidden_zero, my_features(cot_rows_zero, place))
        + over_rows(hidden_one, my_features(cot_rows_one, place))
    ).astype(LOW)
    gain_grad = over_copies((gain_zero + gain_one)[None])[0]

    new_inputs = [act_in[0], input_one]
    guest_new = []
    kept = []
    for m in range(MICRO):
        ids = plan[1, m, plan_row, 1:]
        guest_new.append(
            guests_out(pull_blocks(new_inputs[m], ids, block_width), plan[1, m], section)
        )
        kept.append(clear_blocks(new_inputs[m], ids, block_width, is_early))

    return (
        jnp.stack([front_zero, front_one])[None],
        jnp.stack([d_input_zero, d_input_one])[None],
        jnp.stack(kept)[None],
        jnp.stack(guest_new)[None],
        grad_up[None],
        grad_down[None],
        gain_grad[None],
    )


def solution(mesh):
    placed = (
        P("pipe", ("dp", "tensor"), None),
        P(("dp", "tensor"), None),
        P("pipe", ("dp", "tensor"), None),
        P(("dp", "tensor"), None),
        P("pipe", None, ("dp", "tensor"), None),
        P("pipe", None, None, ("dp", "tensor"), None),
        P(),
        P("pipe", None),
        P("pipe", "dp", "tensor"),
        P("pipe", "tensor", "dp"),
    )
    return jax.shard_map(
        local,
        mesh=mesh,
        in_specs=placed,
        out_specs=(
            P("pipe", None, ("dp", "tensor"), None),
            P("pipe", None, ("dp", "tensor"), None),
            P("pipe", None, ("dp", "tensor"), None),
            P("pipe", None, None, ("dp", "tensor"), None),
            P("pipe", "dp", "tensor"),
            P("pipe", "tensor", "dp"),
            P("pipe", None),
        ),
        check_vma=False,
    )
```

```python
import functools

import jax
import jax.numpy as jnp
from jax import lax
from jax.experimental import pallas as pl
from jax.experimental.pallas import tpu as pltpu
from jax.sharding import PartitionSpec as P

MICRO = 2
EVICT = 3
EPSILON = 1e-05
LOW = jnp.bfloat16
WIDE = jnp.float32

TO_CORE = ("dp", [(d, d ^ 1) for d in range(4)])
TO_Z = ("dp", [(d, d ^ 2) for d in range(4)])
UP_Y = ("tensor", [(t, (t + 1) % 4) for t in range(4)])
DOWN_Y = ("tensor", [(t, (t - 1) % 4) for t in range(4)])
TO_EARLY = ("pipe", [(4 + s, s) for s in range(4)])
TO_LATE = ("pipe", [(s, 4 + s) for s in range(4)])
NEXT = ("pipe", [(s, s + 1) for s in range(7)])
LAST = ("pipe", [(s, s - 1) for s in range(1, 8)])


def round_x(step):
    return ("pipe", [(4 + i, 4 + (i + step) % 4) for i in range(4)])


class Order:
    def __init__(self):
        self.held, self.bulks = None, []

    def send(self, x, route):
        (x,) = self.take(x)
        self.held = x
        return lax.ppermute(x, *route)

    def take(self, *xs):
        if self.held is None:
            return xs
        return lax.optimization_barrier((*xs, self.held))[: len(xs)]

    def send_z(self, x):
        ahead = [(b, i) for b in self.bulks for i in range(b.taken, len(b.landed))]
        return self.send(x, TO_Z), ahead

    def take_z(self, sent):
        x, ahead = sent
        ahead = [(b, i) for b, i in ahead if i >= b.taken]
        values = lax.optimization_barrier((x, self.held, *(b.landed[i] for b, i in ahead)))
        for (b, i), value in zip(ahead, values[2:]):
            b.landed[i], b.taken = value, i + 1
        return values[0]

    def done(self, x):
        (self.held,) = self.take(x)
        return self.held


def call(body, outs, in_smem, *args):
    specs = [pl.BlockSpec(memory_space=pltpu.SMEM)] * in_smem
    specs += [pl.BlockSpec(memory_space=pltpu.VMEM)] * (len(args) - in_smem)
    return pl.pallas_call(
        body,
        out_shape=[jax.ShapeDtypeStruct(*o) for o in outs],
        in_specs=specs,
        out_specs=[pl.BlockSpec(memory_space=pltpu.VMEM)] * len(outs),
        compiler_params=pltpu.CompilerParams(vmem_limit_bytes=32 * 2**20),
    )(*args)


def plan_at(plan_ref, which, tick, row, field):
    return plan_ref[((which * MICRO + tick) * 4 + row) * 4 + field]


def norm_of(values, gain):
    wide = values.astype(WIDE)
    inverse_rms = lax.rsqrt(jnp.mean(wide * wide, axis=-1, keepdims=True) + EPSILON)
    return (wide * inverse_rms * gain).astype(LOW)


def store_split(where_ref, index, values, keep_ref, send_ref):
    half = values.shape[1] // 2
    left, right = values[:, :half], values[:, half:]

    @pl.when(where_ref[1] == 0)
    def _():
        keep_ref[index] = left
        send_ref[index] = right

    @pl.when(where_ref[1] == 1)
    def _():
        keep_ref[index] = right
        send_ref[index] = left


def heads_body(normed, where_ref, gain_ref, *refs):
    *ins, keep_ref, send_ref = refs
    for k, (x, wanted) in enumerate(zip(ins, normed)):
        values = norm_of(x[...], gain_ref[...]) if wanted else x[...]
        store_split(where_ref, k, values, keep_ref, send_ref)


def heads(where, gain, arrays, normed):
    rows, width = arrays[0].shape
    out = ((len(arrays), rows, width // 2), LOW)
    return call(functools.partial(heads_body, normed), [out, out], 1, where, gain, *arrays)


def pick_back_body(where_ref, plan_ref, *refs):
    *around, out = refs
    column = where_ref[0] % 4
    for tick in range(MICRO):
        distance = (plan_at(plan_ref, 0, tick, column, 0) - column + 4) % 4
        for k in range(4):

            @pl.when(distance == k)
            def _(k=k, tick=tick):
                out[tick] = around[k][tick]


def pick_out_body(where_ref, plan_ref, *refs):
    *around, out = refs
    column = where_ref[0] % 4
    out[...] = jnp.zeros_like(out)
    for tick in range(MICRO):
        for k in range(4):
            heading = plan_at(plan_ref, 1, tick, (column + k) % 4, 0) == column

            @pl.when(heading & (where_ref[0] >= 4))
            def _(k=k, tick=tick):
                out[tick] = around[k][tick]


def columns_of(plan_ref, which, tick, row, e, width):
    start = plan_at(plan_ref, which, tick, row, 1 + e) * width
    return pl.ds(pl.multiple_of(start, width), width)


def stash_body(where_ref, plan_ref, gain_ref, own, fetched, old, keep_ref, send_ref):
    width = fetched.shape[-1]
    row = jnp.minimum(where_ref[0], 3)
    for tick in range(MICRO):
        old[tick] = own[tick]

        @pl.when(where_ref[0] < 4)
        def _(tick=tick):
            for e in range(EVICT):
                old[tick, :, columns_of(plan_ref, 0, tick, row, e, width)] = fetched[tick, e]

        store_split(where_ref, tick, norm_of(old[tick], gain_ref[...]), keep_ref, send_ref)


def leave_body(where_ref, plan_ref, first, second, pulled, kept):
    width = pulled.shape[-1]
    row = jnp.minimum(where_ref[0], 3)
    for tick, x in enumerate((first, second)):
        kept[tick] = x[...]
        for e in range(EVICT):
            columns = columns_of(plan_ref, 1, tick, row, e, width)
            pulled[tick, e] = x[:, columns]

            @pl.when(where_ref[0] < 4)
            def _(tick=tick, columns=columns):
                kept[tick, :, columns] = jnp.zeros((kept.shape[1], width), kept.dtype)


def sides(where_ref, keep, got):
    low_z = where_ref[1] == 0
    a, b = keep[...].astype(WIDE), got[...].astype(WIDE)
    return jnp.where(low_z, a, b), jnp.where(low_z, b, a)


def add_body(where_ref, values, keep, got, out):
    half = keep.shape[1]
    left, right = sides(where_ref, keep, got)
    out[:, :half] = (values[:, :half].astype(WIDE) + left).astype(LOW)
    out[:, half:] = (values[:, half:].astype(WIDE) + right).astype(LOW)


def finish_body(where_ref, gain_ref, values, cotangent, keep, got, out, part):
    half = keep.shape[1]
    width = 2 * half
    wide = values[...].astype(WIDE)
    inverse_rms = lax.rsqrt(jnp.mean(wide * wide, axis=-1, keepdims=True) + EPSILON)
    cubed = inverse_rms * inverse_rms * inverse_rms
    pieces = []
    for at, d_normed in zip((0, half), sides(where_ref, keep, got)):
        columns = slice(at, at + half)
        v = values[:, columns].astype(WIDE)
        part[:, columns] = jnp.sum(d_normed * v * inverse_rms, axis=0, keepdims=True)
        scaled = d_normed * gain_ref[:, columns]
        pieces.append((columns, v, scaled, jnp.sum(scaled * v, axis=-1, keepdims=True)))
    mean = (pieces[0][3] + pieces[1][3]) / width
    for columns, v, scaled, _ in pieces:
        g = cotangent[:, columns].astype(WIDE)
        out[:, columns] = (g + inverse_rms * scaled - v * cubed * mean).astype(LOW)


def ordered(at_zero, own, other):
    return jnp.where(at_zero, own, other), jnp.where(at_zero, other, own)


class Gather:
    def __init__(self, order, low_z, keep, send):
        self.order, self.low_z, self.keep, self.outgoing = order, low_z, keep, send

    def z(self):
        self.got = self.order.send_z(self.outgoing)

    def y(self):
        self.got = self.order.take_z(self.got)
        self.mine = jnp.stack(ordered(self.low_z, self.keep, self.got))
        self.before = self.order.send(self.mine, UP_Y)
        self.behind = self.order.send(self.mine, DOWN_Y)

    def far(self):
        self.before, self.behind = self.order.take(self.before, self.behind)
        self.far_low = self.order.send(self.before[0], UP_Y)
        self.far_high = self.order.send(self.behind[1], DOWN_Y)

    def core(self):
        self.far_low, self.far_high = self.order.take(self.far_low, self.far_high)
        self.ring = [
            jnp.stack(
                [
                    self.mine[:, k],
                    self.behind[:, k],
                    jnp.stack([self.far_low[k], self.far_high[k]]),
                    self.before[:, k],
                ]
            )
            for k in range(self.keep.shape[0])
        ]
        self.swapped = [self.order.send(r, TO_CORE) for r in self.ring]

    def rows(self):
        half = self.keep.shape[-1]
        self.swapped = self.order.take(*self.swapped)
        return [
            jnp.concatenate([r, s]).reshape(-1, half) for r, s in zip(self.ring, self.swapped)
        ]


class Settle:
    def __init__(self, order, low_z):
        self.order, self.low_z = order, low_z

    def core(self, part):
        half = part.shape[0] // 2
        self.kept = part[:half]
        self.got = self.order.send(part[half:].astype(LOW), TO_CORE)

    def far(self):
        half, width = self.kept.shape
        (self.got,) = self.order.take(self.got)
        self.summed = (self.kept + self.got.astype(WIDE)).reshape(4, 2, half // 8, width)
        self.low = self.order.send(self.summed[2, 0].astype(LOW), UP_Y)
        self.high = self.order.send(self.summed[2, 1].astype(LOW), DOWN_Y)

    def y(self):
        s = self.summed
        self.low, self.high = self.order.take(self.low, self.high)
        up = jnp.stack([s[1, 0] + self.low.astype(WIDE), s[1, 1]]).astype(LOW)
        down = jnp.stack([s[3, 0], s[3, 1] + self.high.astype(WIDE)]).astype(LOW)
        self.first = self.order.send(up, UP_Y)
        self.second = self.order.send(down, DOWN_Y)

    def z(self):
        self.first, self.second = self.order.take(self.first, self.second)
        mine = self.summed[0] + self.first.astype(WIDE) + self.second.astype(WIDE)
        mine = mine.astype(LOW)
        self.keep = jnp.where(self.low_z, mine[0], mine[1])
        self.got = self.order.send_z(jnp.where(self.low_z, mine[1], mine[0]))

    def end(self):
        self.got = self.order.take_z(self.got)
        return self.keep, self.got


class Bulk:
    def __init__(self, order, part, chunks):
        self.order, self.own = order, part.astype(LOW)
        self.size = part.shape[0] // chunks
        self.landed, self.taken = [], 0
        order.bulks.append(self)

    def z(self):
        at = len(self.landed) * self.size
        self.landed.append(self.order.send(self.own[at : at + self.size], TO_Z))

    def take(self):
        i = self.taken
        (self.landed[i],) = self.order.take(self.landed[i])
        self.taken = i + 1

    def total(self):
        self.landed = list(self.order.take(*self.landed))
        self.taken = len(self.landed)
        got = self.landed[0] if len(self.landed) == 1 else jnp.concatenate(self.landed)
        return self.own.astype(WIDE) + got.astype(WIDE)


def times(a, b):
    return jnp.dot(a, b, preferred_element_type=WIDE)


def times_transposed(a, b):
    return lax.dot_general(a, b, (((1,), (1,)), ((), ())), preferred_element_type=WIDE)


def over_rows(a, b):
    return lax.dot_general(a, b, (((0,), (0,)), ((), ())), preferred_element_type=WIDE)


def activations(hidden_pre, d_hidden):
    gate = jax.nn.sigmoid(hidden_pre)
    hidden = (hidden_pre * gate).astype(LOW)
    return hidden, (d_hidden * gate * (1.0 + hidden_pre * (1.0 - gate))).astype(LOW)


def local(
    act_in, act_first, grad_in, grad_last, stash_local, stash_guest, plan, norm_gain, w_up, w_down
):
    order = Order()
    section, d = lax.axis_index("pipe"), lax.axis_index("dp")
    z, core = d // 2, d % 2
    low_z, low_core = z == 0, core == 0
    where = jnp.stack([section, z]).astype(jnp.int32)
    plan = plan.reshape(-1)
    rows, width = act_in.shape[1:]
    whole = ((rows, width), LOW)
    parcel = (stash_guest.shape[1:], LOW)

    def gather(keep, send):
        return Gather(order, low_z, keep, send)

    def swap_hidden(*owns):
        return [(own, order.send(own, TO_CORE)) for own in owns]

    def whole_hidden(*pairs):
        wholes = []
        for own, got in pairs:
            (got,) = order.take(got)
            half = own.shape[0] // 2
            other = jnp.concatenate([got[half:], got[:half]])
            wholes.append(order.done(jnp.concatenate(ordered(low_core, own, other), axis=1)))
        return wholes

    def my_features(x):
        half = x.shape[1] // 2
        return jnp.where(low_core, x[:, :half], x[:, half:])

    def finished(values, cotangent, settled):
        outs = [whole, ((1, width), WIDE)]
        args = (where, norm_gain, values, cotangent, *settled.end())
        return call(finish_body, outs, 1, *args)

    held = stash_guest[0]
    around = [held] + [order.send(held, round_x(step)) for step in (-1, -2, 1)]
    first = gather(*heads(where, norm_gain, [grad_in[0], act_in[0]], (False, True)))
    first.z()

    w_up, w_down = order.take(w_up, w_down)
    half = w_up.shape[2] // 2
    here, there = core * half, (1 - core) * half
    down_got = order.send(lax.dynamic_slice_in_dim(w_down[0], there, half, 0), TO_CORE)
    (found,) = call(pick_back_body, [parcel], 2, where, plan, *order.take(*around))
    guests = order.send(found, TO_EARLY)
    first.y()
    up_got = order.send(lax.dynamic_slice_in_dim(w_up[0], there, half, 1), TO_CORE)
    (down_got,) = order.take(down_got)
    down_own = lax.dynamic_slice_in_dim(w_down[0], here, half, 0)
    down = order.done(jnp.concatenate(ordered(low_core, down_own, down_got), axis=1))
    first.far()
    (up_got,) = order.take(up_got)
    up_own = lax.dynamic_slice_in_dim(w_up[0], here, half, 1)
    up = order.done(jnp.concatenate(ordered(low_core, up_own, up_got), axis=0))

    pair = ((MICRO, rows, width // 2), LOW)
    old, *split = call(
        stash_body,
        [((MICRO, rows, width), LOW), pair, pair],
        2,
        where,
        plan,
        norm_gain,
        stash_local[0],
        *order.take(guests),
    )
    stash = gather(*split)
    stash.z()
    first.core()
    cot_rows_zero, front_rows_zero = first.rows()
    stash.y()
    d_hidden_zero = Bulk(order, times_transposed(cot_rows_zero, down), 1)
    d_hidden_zero.z()
    stash.far()
    stash.core()
    stash_rows = stash.rows()
    pre_zero = Bulk(order, times(stash_rows[0], up), 1)
    pre_zero.z()
    front_pre_zero = Bulk(order, times(front_rows_zero, up), 2)
    front_pre_zero.z()
    pre_one = Bulk(order, order.done(times(stash_rows[1], up).astype(LOW)), 2)

    hidden_zero, d_pre_zero = activations(pre_zero.total(), d_hidden_zero.total())
    back = Settle(order, low_z)
    back.core(times_transposed(d_pre_zero, up))
    front_pre_zero.z()
    front_pre_zero.take()
    back.far()
    back.y()
    back.z()
    pre_one.z()
    hidden_zero, d_pre_zero = swap_hidden(hidden_zero, d_pre_zero)
    d_input_zero, gain_zero = finished(old[0], grad_in[0], back)
    returned = order.send(d_input_zero, LAST)

    front = Settle(order, low_z)
    front_hidden = jax.nn.silu(front_pre_zero.total()).astype(LOW)
    front.core(times(front_hidden, down))
    cot_one = jnp.where(section == 7, grad_last, order.take(returned)[0])
    second = gather(*heads(where, norm_gain, [cot_one], (False,)))
    second.z()
    pre_one.z()
    front.far()
    second.y()
    front.y()
    second.far()
    front.z()
    second.core()
    (cot_rows_one,) = second.rows()
    d_hidden_one = Bulk(order, times_transposed(cot_rows_one, down), 2)
    d_hidden_one.z()
    (front_zero,) = call(add_body, [whole], 1, where, act_in[0], *front.end())
    passed = order.send(front_zero, NEXT)
    hidden_zero, d_pre_zero = whole_hidden(hidden_zero, d_pre_zero)
    grad_up = order.done(over_rows(my_features(stash_rows[0]), d_pre_zero))
    input_one = jnp.where(section == 0, act_first, order.take(passed)[0])
    third = gather(*heads(where, norm_gain, [input_one], (True,)))
    third.z()
    d_hidden_one.z()
    pulled, kept = call(
        leave_body,
        [parcel, ((MICRO, rows, width), LOW)],
        2,
        where,
        plan,
        act_in[0],
        input_one,
    )
    third.y()
    landed = order.send(pulled, TO_LATE)
    grad_down = order.done(over_rows(hidden_zero, my_features(cot_rows_zero)))
    third.far()
    third.core()
    (front_rows_one,) = third.rows()
    (landed,) = order.take(landed)
    front_pre_one = Bulk(order, order.done(times(front_rows_one, up).astype(LOW)), 1)
    front_pre_one.z()

    hidden_one, d_pre_one = activations(pre_one.total(), d_hidden_one.total())
    back = Settle(order, low_z)
    back.core(times_transposed(d_pre_one, up))
    hidden_one, d_pre_one = swap_hidden(hidden_one, d_pre_one)
    back.far()
    around = [landed] + [order.send(landed, round_x(step)) for step in (-1, -2, 1)]
    back.y()
    hidden_one, d_pre_one = whole_hidden(hidden_one, d_pre_one)
    back.z()
    (guest_new,) = call(pick_out_body, [parcel], 2, where, plan, *order.take(*around))
    more = over_rows(my_features(stash_rows[1]), d_pre_one)
    grad_up = order.done((grad_up + more).astype(LOW))
    more = over_rows(hidden_one, my_features(cot_rows_one))
    grad_down = order.done((grad_down + more).astype(LOW))

    front = Settle(order, low_z)
    front_hidden = jax.nn.silu(front_pre_one.total()).astype(LOW)
    front.core(times(front_hidden, down))
    d_input_one, gain_one = finished(old[1], cot_one, back)
    gain = gain_zero + gain_one
    gain = gain + order.send(gain, TO_CORE)
    front.far()
    gain = gain + order.send(gain, TO_Z)
    front.y()
    gain = gain + order.send(gain, ("tensor", [(t, t ^ 1) for t in range(4)]))
    front.z()
    gain = gain + order.send(gain, ("tensor", [(t, t ^ 2) for t in range(4)]))
    (front_one,) = call(add_body, [whole], 1, where, input_one, *front.end())

    return (
        jnp.stack([front_zero, front_one])[None],
        jnp.stack([d_input_zero, d_input_one])[None],
        kept[None],
        guest_new[None],
        grad_up[None],
        grad_down[None],
        gain,
    )


def solution(mesh):
    placed = (
        P("pipe", ("dp", "tensor"), None),
        P(("dp", "tensor"), None),
        P("pipe", ("dp", "tensor"), None),
        P(("dp", "tensor"), None),
        P("pipe", None, ("dp", "tensor"), None),
        P("pipe", None, None, ("dp", "tensor"), None),
        P(),
        P("pipe", None),
        P("pipe", "dp", "tensor"),
        P("pipe", "tensor", "dp"),
    )
    return jax.shard_map(
        local,
        mesh=mesh,
        in_specs=placed,
        out_specs=(
            P("pipe", None, ("dp", "tensor"), None),
            P("pipe", None, ("dp", "tensor"), None),
            P("pipe", None, ("dp", "tensor"), None),
            P("pipe", None, None, ("dp", "tensor"), None),
            P("pipe", "dp", "tensor"),
            P("pipe", "tensor", "dp"),
            P("pipe", None),
        ),
        check_vma=False,
    )
```

```python
import functools

import jax
import jax.numpy as jnp
from jax import lax
from jax.experimental import pallas as pl
from jax.experimental.pallas import tpu as pltpu
from jax.sharding import PartitionSpec as P

MICRO = 2
EVICT = 3
EPSILON = 1e-05
LOW = jnp.bfloat16
WIDE = jnp.float32

TO_CORE = ("dp", [(d, d ^ 1) for d in range(4)])
TO_Z = ("dp", [(d, d ^ 2) for d in range(4)])
UP_Y = ("tensor", [(t, (t + 1) % 4) for t in range(4)])
DOWN_Y = ("tensor", [(t, (t - 1) % 4) for t in range(4)])
TO_EARLY = ("pipe", [(4 + s, s) for s in range(4)])
TO_LATE = ("pipe", [(s, 4 + s) for s in range(4)])
NEXT = ("pipe", [(s, s + 1) for s in range(7)])
LAST = ("pipe", [(s, s - 1) for s in range(1, 8)])


def round_x(step):
    return ("pipe", [(4 + i, 4 + (i + step) % 4) for i in range(4)])


class Order:
    def __init__(self):
        self.held, self.bulks = None, []

    def send(self, x, route):
        (x,) = self.take(x)
        self.held = x
        return lax.ppermute(x, *route)

    def send_both_ways(self, up, down):
        same = up is down
        if same:
            (up,) = self.take(up)
            down = up
        else:
            up, down = self.take(up, down)
        self.held = down
        return lax.ppermute(up, *UP_Y), lax.ppermute(down, *DOWN_Y)

    def tie(self, x):
        x, self.held = lax.optimization_barrier((x, self.held))
        return x

    def take(self, *xs):
        if self.held is None:
            return xs
        return lax.optimization_barrier((*xs, self.held))[: len(xs)]

    def send_z(self, x):
        ahead = [(b, i) for b in self.bulks for i in range(b.taken, len(b.landed))]
        return self.send(x, TO_Z), ahead

    def take_z(self, sent):
        x, ahead = sent
        ahead = [(b, i) for b, i in ahead if i >= b.taken]
        values = lax.optimization_barrier((x, self.held, *(b.landed[i] for b, i in ahead)))
        for (b, i), value in zip(ahead, values[2:]):
            b.landed[i], b.taken = value, i + 1
        return values[0]

    def done(self, x):
        (self.held,) = self.take(x)
        return self.held


def call(body, outs, in_smem, *args):
    specs = [pl.BlockSpec(memory_space=pltpu.SMEM)] * in_smem
    specs += [pl.BlockSpec(memory_space=pltpu.VMEM)] * (len(args) - in_smem)
    return pl.pallas_call(
        body,
        out_shape=[jax.ShapeDtypeStruct(*o) for o in outs],
        in_specs=specs,
        out_specs=[pl.BlockSpec(memory_space=pltpu.VMEM)] * len(outs),
        compiler_params=pltpu.CompilerParams(vmem_limit_bytes=32 * 2**20),
    )(*args)


def plan_at(plan_ref, which, tick, row, field):
    return plan_ref[((which * MICRO + tick) * 4 + row) * 4 + field]


def norm_of(values, gain):
    wide = values.astype(WIDE)
    inverse_rms = lax.rsqrt(jnp.mean(wide * wide, axis=-1, keepdims=True) + EPSILON)
    return (wide * inverse_rms * gain).astype(LOW)


def store_split(where_ref, index, values, keep_ref, send_ref):
    half = values.shape[1] // 2
    left, right = values[:, :half], values[:, half:]

    @pl.when(where_ref[1] == 0)
    def _():
        keep_ref[index] = left
        send_ref[index] = right

    @pl.when(where_ref[1] == 1)
    def _():
        keep_ref[index] = right
        send_ref[index] = left


def heads_body(normed, where_ref, gain_ref, *refs):
    *ins, keep_ref, send_ref = refs
    for k, (x, wanted) in enumerate(zip(ins, normed)):
        values = norm_of(x[...], gain_ref[...]) if wanted else x[...]
        store_split(where_ref, k, values, keep_ref, send_ref)


def heads(where, gain, arrays, normed):
    rows, width = arrays[0].shape
    out = ((len(arrays), rows, width // 2), LOW)
    return call(functools.partial(heads_body, normed), [out, out], 1, where, gain, *arrays)


def pick_back_body(where_ref, plan_ref, *refs):
    *around, out = refs
    column = where_ref[0] % 4
    for tick in range(MICRO):
        distance = (plan_at(plan_ref, 0, tick, column, 0) - column + 4) % 4
        for k in range(4):

            @pl.when(distance == k)
            def _(k=k, tick=tick):
                out[tick] = around[k][tick]


def pick_out_body(where_ref, plan_ref, *refs):
    *around, out = refs
    column = where_ref[0] % 4
    out[...] = jnp.zeros_like(out)
    for tick in range(MICRO):
        for k in range(4):
            heading = plan_at(plan_ref, 1, tick, (column + k) % 4, 0) == column

            @pl.when(heading & (where_ref[0] >= 4))
            def _(k=k, tick=tick):
                out[tick] = around[k][tick]


def columns_of(plan_ref, which, tick, row, e, width):
    start = plan_at(plan_ref, which, tick, row, 1 + e) * width
    return pl.ds(pl.multiple_of(start, width), width)


def stash_body(where_ref, plan_ref, gain_ref, own, fetched, old, keep_ref, send_ref):
    width = fetched.shape[-1]
    row = jnp.minimum(where_ref[0], 3)
    for tick in range(MICRO):
        old[tick] = own[tick]

        @pl.when(where_ref[0] < 4)
        def _(tick=tick):
            for e in range(EVICT):
                old[tick, :, columns_of(plan_ref, 0, tick, row, e, width)] = fetched[tick, e]

        store_split(where_ref, tick, norm_of(old[tick], gain_ref[...]), keep_ref, send_ref)


def leave_body(where_ref, plan_ref, first, second, pulled, kept):
    width = pulled.shape[-1]
    row = jnp.minimum(where_ref[0], 3)
    for tick, x in enumerate((first, second)):
        kept[tick] = x[...]
        for e in range(EVICT):
            columns = columns_of(plan_ref, 1, tick, row, e, width)
            pulled[tick, e] = x[:, columns]

            @pl.when(where_ref[0] < 4)
            def _(tick=tick, columns=columns):
                kept[tick, :, columns] = jnp.zeros((kept.shape[1], width), kept.dtype)


def sides(where_ref, keep, got):
    low_z = where_ref[1] == 0
    a, b = keep[...].astype(WIDE), got[...].astype(WIDE)
    return jnp.where(low_z, a, b), jnp.where(low_z, b, a)


def add_body(where_ref, values, keep, got, out):
    half = keep.shape[1]
    left, right = sides(where_ref, keep, got)
    out[:, :half] = (values[:, :half].astype(WIDE) + left).astype(LOW)
    out[:, half:] = (values[:, half:].astype(WIDE) + right).astype(LOW)


def finish_body(where_ref, gain_ref, values, cotangent, keep, got, out, part):
    half = keep.shape[1]
    width = 2 * half
    wide = values[...].astype(WIDE)
    inverse_rms = lax.rsqrt(jnp.mean(wide * wide, axis=-1, keepdims=True) + EPSILON)
    cubed = inverse_rms * inverse_rms * inverse_rms
    pieces = []
    for at, d_normed in zip((0, half), sides(where_ref, keep, got)):
        columns = slice(at, at + half)
        v = values[:, columns].astype(WIDE)
        part[:, columns] = jnp.sum(d_normed * v * inverse_rms, axis=0, keepdims=True)
        scaled = d_normed * gain_ref[:, columns]
        pieces.append((columns, v, scaled, jnp.sum(scaled * v, axis=-1, keepdims=True)))
    mean = (pieces[0][3] + pieces[1][3]) / width
    for columns, v, scaled, _ in pieces:
        g = cotangent[:, columns].astype(WIDE)
        out[:, columns] = (g + inverse_rms * scaled - v * cubed * mean).astype(LOW)


def ordered(at_zero, own, other):
    return jnp.where(at_zero, own, other), jnp.where(at_zero, other, own)


class Gather:
    def __init__(self, order, low_z, keep, send):
        self.order, self.low_z, self.keep, self.outgoing = order, low_z, keep, send

    def z(self):
        self.got = self.order.send_z(self.outgoing)

    def y(self):
        self.got = self.order.take_z(self.got)
        self.mine = jnp.stack(ordered(self.low_z, self.keep, self.got))
        self.before, self.behind = self.order.send_both_ways(self.mine, self.mine)

    def far(self):
        self.before, self.behind = self.order.take(self.before, self.behind)
        both = self.order.send_both_ways(self.before[0], self.behind[1])
        self.far_low, self.far_high = both

    def core(self):
        self.far_low, self.far_high = self.order.take(self.far_low, self.far_high)
        self.ring = [
            jnp.stack(
                [
                    self.mine[:, k],
                    self.behind[:, k],
                    jnp.stack([self.far_low[k], self.far_high[k]]),
                    self.before[:, k],
                ]
            )
            for k in range(self.keep.shape[0])
        ]
        self.swapped = [self.order.send(r, TO_CORE) for r in self.ring]

    def rows(self):
        half = self.keep.shape[-1]
        self.swapped = self.order.take(*self.swapped)
        return [
            jnp.concatenate([r, s]).reshape(-1, half) for r, s in zip(self.ring, self.swapped)
        ]


class Settle:
    def __init__(self, order, low_z):
        self.order, self.low_z = order, low_z

    def core(self, part):
        half = part.shape[0] // 2
        self.kept = part[:half]
        self.got = self.order.send(part[half:].astype(LOW), TO_CORE)

    def far(self):
        half, width = self.kept.shape
        (self.got,) = self.order.take(self.got)
        self.summed = (self.kept + self.got.astype(WIDE)).reshape(4, 2, half // 8, width)
        far = self.summed[2].astype(LOW)
        self.low, self.high = self.order.send_both_ways(far[0], far[1])

    def y(self):
        s = self.summed
        self.low, self.high = self.order.take(self.low, self.high)
        up = jnp.stack([s[1, 0] + self.low.astype(WIDE), s[1, 1]]).astype(LOW)
        down = jnp.stack([s[3, 0], s[3, 1] + self.high.astype(WIDE)]).astype(LOW)
        self.first, self.second = self.order.send_both_ways(up, down)

    def z(self):
        self.first, self.second = self.order.take(self.first, self.second)
        mine = self.summed[0] + self.first.astype(WIDE) + self.second.astype(WIDE)
        mine = mine.astype(LOW)
        self.keep = jnp.where(self.low_z, mine[0], mine[1])
        self.got = self.order.send_z(jnp.where(self.low_z, mine[1], mine[0]))

    def end(self):
        self.got = self.order.take_z(self.got)
        return self.keep, self.got


class Bulk:
    def __init__(self, order, part, chunks):
        self.order, self.own = order, part.astype(LOW)
        self.size = part.shape[0] // chunks
        self.landed, self.taken = [], 0
        order.bulks.append(self)

    def z(self):
        at = len(self.landed) * self.size
        self.landed.append(self.order.send(self.own[at : at + self.size], TO_Z))

    def take(self):
        i = self.taken
        self.landed[i] = self.order.tie(self.landed[i])
        self.taken = i + 1

    def total(self):
        self.landed = list(self.order.take(*self.landed))
        self.taken = len(self.landed)
        got = self.landed[0] if len(self.landed) == 1 else jnp.concatenate(self.landed)
        return self.own.astype(WIDE) + got.astype(WIDE)


def times(a, b):
    return jnp.dot(a, b, preferred_element_type=WIDE)


def times_transposed(a, b):
    return lax.dot_general(a, b, (((1,), (1,)), ((), ())), preferred_element_type=WIDE)


def over_rows(a, b):
    return lax.dot_general(a, b, (((0,), (0,)), ((), ())), preferred_element_type=WIDE)


def activations(hidden_pre, d_hidden):
    gate = jax.nn.sigmoid(hidden_pre)
    hidden = (hidden_pre * gate).astype(LOW)
    return hidden, (d_hidden * gate * (1.0 + hidden_pre * (1.0 - gate))).astype(LOW)


def local(
    act_in, act_first, grad_in, grad_last, stash_local, stash_guest, plan, norm_gain, w_up, w_down
):
    order = Order()
    section, d = lax.axis_index("pipe"), lax.axis_index("dp")
    z, core = d // 2, d % 2
    low_z, low_core = z == 0, core == 0
    where = jnp.stack([section, z]).astype(jnp.int32)
    plan = plan.reshape(-1)
    rows, width = act_in.shape[1:]
    whole = ((rows, width), LOW)
    parcel = (stash_guest.shape[1:], LOW)

    def gather(keep, send):
        return Gather(order, low_z, keep, send)

    def swap_hidden(*owns):
        return [(own, order.send(own, TO_CORE)) for own in owns]

    def whole_hidden(*pairs):
        wholes = []
        for own, got in pairs:
            (got,) = order.take(got)
            half = own.shape[0] // 2
            other = jnp.concatenate([got[half:], got[:half]])
            wholes.append(order.done(jnp.concatenate(ordered(low_core, own, other), axis=1)))
        return wholes

    def my_features(x):
        half = x.shape[1] // 2
        return jnp.where(low_core, x[:, :half], x[:, half:])

    def finished(values, cotangent, settled):
        outs = [whole, ((1, width), WIDE)]
        args = (where, norm_gain, values, cotangent, *settled.end())
        return call(finish_body, outs, 1, *args)

    first = gather(*heads(where, norm_gain, [grad_in[0], act_in[0]], (False, True)))
    first.z()
    held = stash_guest[0]
    around = [held] + [order.send(held, round_x(step)) for step in (-1, -2, 1)]

    (found,) = call(pick_back_body, [parcel], 2, where, plan, *order.take(*around))
    guests = order.send(found, TO_EARLY)
    first.y()
    w_up, w_down = order.take(w_up, w_down)
    half = w_up.shape[2] // 2
    here, there = core * half, (1 - core) * half
    down_got = order.send(lax.dynamic_slice_in_dim(w_down[0], there, half, 0), TO_CORE)
    up_got = order.send(lax.dynamic_slice_in_dim(w_up[0], there, half, 1), TO_CORE)
    (down_got,) = order.take(down_got)
    down_own = lax.dynamic_slice_in_dim(w_down[0], here, half, 0)
    down = order.done(jnp.concatenate(ordered(low_core, down_own, down_got), axis=1))
    first.far()
    (up_got,) = order.take(up_got)
    up_own = lax.dynamic_slice_in_dim(w_up[0], here, half, 1)
    up = order.done(jnp.concatenate(ordered(low_core, up_own, up_got), axis=0))

    pair = ((MICRO, rows, width // 2), LOW)
    old, *split = call(
        stash_body,
        [((MICRO, rows, width), LOW), pair, pair],
        2,
        where,
        plan,
        norm_gain,
        stash_local[0],
        *order.take(guests),
    )
    stash = gather(*split)
    stash.z()
    first.core()
    cot_rows_zero, front_rows_zero = first.rows()
    stash.y()
    d_hidden_zero = Bulk(order, times_transposed(cot_rows_zero, down), 1)
    d_hidden_zero.z()
    stash.far()
    stash.core()
    stash_rows = stash.rows()
    pre_zero = Bulk(order, times(stash_rows[0], up), 1)
    pre_zero.z()
    front_pre_zero = Bulk(order, times(front_rows_zero, up), 4)
    front_pre_zero.z()
    pre_one = Bulk(order, order.done(times(stash_rows[1], up).astype(LOW)), 2)

    hidden_zero, d_pre_zero = activations(pre_zero.total(), d_hidden_zero.total())
    back = Settle(order, low_z)
    d_rows = order.done(times_transposed(d_pre_zero, up))
    front_pre_zero.z()
    front_pre_zero.take()
    back.core(d_rows)
    front_pre_zero.z()
    front_pre_zero.take()
    back.far()
    front_pre_zero.z()
    front_pre_zero.take()
    back.y()
    back.z()
    hidden_zero, d_pre_zero = swap_hidden(hidden_zero, d_pre_zero)
    d_input_zero, gain_zero = finished(old[0], grad_in[0], back)
    returned = order.send(d_input_zero, LAST)

    front = Settle(order, low_z)
    front_hidden = jax.nn.silu(front_pre_zero.total()).astype(LOW)
    front.core(times(front_hidden, down))
    cot_one = jnp.where(section == 7, grad_last, order.take(returned)[0])
    second = gather(*heads(where, norm_gain, [cot_one], (False,)))
    second.z()
    pre_one.z()
    pre_one.z()
    front.far()
    second.y()
    front.y()
    second.far()
    front.z()
    second.core()
    (cot_rows_one,) = second.rows()
    d_hidden_one = Bulk(order, times_transposed(cot_rows_one, down), 2)
    d_hidden_one.z()
    (front_zero,) = call(add_body, [whole], 1, where, act_in[0], *front.end())
    passed = order.send(front_zero, NEXT)
    hidden_zero, d_pre_zero = whole_hidden(hidden_zero, d_pre_zero)
    grad_up = order.done(over_rows(my_features(stash_rows[0]), d_pre_zero))
    input_one = jnp.where(section == 0, act_first, order.take(passed)[0])
    third = gather(*heads(where, norm_gain, [input_one], (True,)))
    third.z()
    d_hidden_one.z()
    pulled, kept = call(
        leave_body,
        [parcel, ((MICRO, rows, width), LOW)],
        2,
        where,
        plan,
        act_in[0],
        input_one,
    )
    landed = order.send(pulled, TO_LATE)
    third.y()
    grad_down = order.done(over_rows(hidden_zero, my_features(cot_rows_zero)))
    third.far()
    landed = order.tie(landed)
    third.core()
    (front_rows_one,) = third.rows()
    part = order.done(times(front_rows_one, up).astype(LOW))
    front_pre_one = Bulk(order, part, 4)
    front_pre_one.z()
    front_pre_one.z()

    hidden_one, d_pre_one = activations(pre_one.total(), d_hidden_one.total())
    back = Settle(order, low_z)
    d_rows = order.done(times_transposed(d_pre_one, up))
    back.core(d_rows)
    hidden_one, d_pre_one = swap_hidden(hidden_one, d_pre_one)
    around = [landed] + [order.send(landed, round_x(step)) for step in (-1, -2, 1)]
    front_pre_one.take()
    front_pre_one.z()
    hidden_one, d_pre_one = whole_hidden(hidden_one, d_pre_one)
    more = over_rows(my_features(stash_rows[1]), d_pre_one)
    grad_up = order.done((grad_up + more).astype(LOW))
    front_pre_one.take()
    front_pre_one.z()
    back.far()
    (guest_new,) = call(pick_out_body, [parcel], 2, where, plan, *order.take(*around))
    guest_new = order.done(guest_new)
    more = over_rows(hidden_one, my_features(cot_rows_one))
    grad_down = order.done((grad_down + more).astype(LOW))
    front_pre_one.take()
    back.y()
    front_pre_one.take()

    front = Settle(order, low_z)
    front_hidden = jax.nn.silu(front_pre_one.total()).astype(LOW)
    front.core(times(front_hidden, down))
    back.z()
    d_input_one, gain_one = finished(old[1], cot_one, back)
    gain = gain_zero + gain_one
    gain = gain + order.send(gain, TO_CORE)
    front.far()
    gain = gain + order.send(gain, TO_Z)
    front.y()
    gain = gain + order.send(gain, ("tensor", [(t, t ^ 1) for t in range(4)]))
    front.z()
    gain = gain + order.send(gain, ("tensor", [(t, t ^ 2) for t in range(4)]))
    (front_one,) = call(add_body, [whole], 1, where, input_one, *front.end())

    return (
        jnp.stack([front_zero, front_one])[None],
        jnp.stack([d_input_zero, d_input_one])[None],
        kept[None],
        guest_new[None],
        grad_up[None],
        grad_down[None],
        gain,
    )


def solution(mesh):
    placed = (
        P("pipe", ("dp", "tensor"), None),
        P(("dp", "tensor"), None),
        P("pipe", ("dp", "tensor"), None),
        P(("dp", "tensor"), None),
        P("pipe", None, ("dp", "tensor"), None),
        P("pipe", None, None, ("dp", "tensor"), None),
        P(),
        P("pipe", None),
        P("pipe", "dp", "tensor"),
        P("pipe", "tensor", "dp"),
    )
    return jax.shard_map(
        local,
        mesh=mesh,
        in_specs=placed,
        out_specs=(
            P("pipe", None, ("dp", "tensor"), None),
            P("pipe", None, ("dp", "tensor"), None),
            P("pipe", None, ("dp", "tensor"), None),
            P("pipe", None, None, ("dp", "tensor"), None),
            P("pipe", "dp", "tensor"),
            P("pipe", "tensor", "dp"),
            P("pipe", None),
        ),
        check_vma=False,
    )
```

```python
import functools

import jax
import jax.numpy as jnp
from jax import lax
from jax.experimental import pallas as pl
from jax.experimental.pallas import tpu as pltpu
from jax.sharding import PartitionSpec as P

MICRO = 2
EVICT = 3
EPSILON = 1e-05
LOW = jnp.bfloat16
WIDE = jnp.float32

TO_CORE = ("dp", [(d, d ^ 1) for d in range(4)])
TO_Z = ("dp", [(d, d ^ 2) for d in range(4)])
UP_Y = ("tensor", [(t, (t + 1) % 4) for t in range(4)])
DOWN_Y = ("tensor", [(t, (t - 1) % 4) for t in range(4)])
TO_EARLY = ("pipe", [(4 + s, s) for s in range(4)])
TO_LATE = ("pipe", [(s, 4 + s) for s in range(4)])
NEXT = ("pipe", [(s, s + 1) for s in range(7)])
LAST = ("pipe", [(s, s - 1) for s in range(1, 8)])


def round_x(step):
    return ("pipe", [(4 + i, 4 + (i + step) % 4) for i in range(4)])


class Order:
    def __init__(self):
        self.held, self.bulks = None, []

    def send(self, x, route):
        (x,) = self.take(x)
        self.held = x
        return lax.ppermute(x, *route)

    def send_both_ways(self, up, down):
        same = up is down
        if same:
            (up,) = self.take(up)
            down = up
        else:
            up, down = self.take(up, down)
        self.held = down
        return lax.ppermute(up, *UP_Y), lax.ppermute(down, *DOWN_Y)

    def tie(self, x):
        x, self.held = lax.optimization_barrier((x, self.held))
        return x

    def take(self, *xs):
        if self.held is None:
            return xs
        return lax.optimization_barrier((*xs, self.held))[: len(xs)]

    def send_z(self, x):
        ahead = [(b, i) for b in self.bulks for i in range(b.taken, len(b.landed))]
        return self.send(x, TO_Z), ahead

    def take_z(self, sent):
        x, ahead = sent
        ahead = [(b, i) for b, i in ahead if i >= b.taken]
        values = lax.optimization_barrier((x, self.held, *(b.landed[i] for b, i in ahead)))
        for (b, i), value in zip(ahead, values[2:]):
            b.landed[i], b.taken = value, i + 1
        return values[0]

    def done(self, x):
        (self.held,) = self.take(x)
        return self.held


def call(body, outs, in_smem, *args):
    specs = [pl.BlockSpec(memory_space=pltpu.SMEM)] * in_smem
    specs += [pl.BlockSpec(memory_space=pltpu.VMEM)] * (len(args) - in_smem)
    return pl.pallas_call(
        body,
        out_shape=[jax.ShapeDtypeStruct(*o) for o in outs],
        in_specs=specs,
        out_specs=[pl.BlockSpec(memory_space=pltpu.VMEM)] * len(outs),
        compiler_params=pltpu.CompilerParams(vmem_limit_bytes=32 * 2**20),
    )(*args)


def plan_at(plan_ref, which, tick, row, field):
    return plan_ref[((which * MICRO + tick) * 4 + row) * 4 + field]


def norm_of(values, gain):
    wide = values.astype(WIDE)
    inverse_rms = lax.rsqrt(jnp.mean(wide * wide, axis=-1, keepdims=True) + EPSILON)
    return (wide * inverse_rms * gain).astype(LOW)


def store_split(where_ref, index, values, keep_ref, send_ref):
    half = values.shape[1] // 2
    left, right = values[:, :half], values[:, half:]

    @pl.when(where_ref[1] == 0)
    def _():
        keep_ref[index] = left
        send_ref[index] = right

    @pl.when(where_ref[1] == 1)
    def _():
        keep_ref[index] = right
        send_ref[index] = left


def heads_body(normed, where_ref, gain_ref, *refs):
    *ins, keep_ref, send_ref = refs
    for k, (x, wanted) in enumerate(zip(ins, normed)):
        values = norm_of(x[...], gain_ref[...]) if wanted else x[...]
        store_split(where_ref, k, values, keep_ref, send_ref)


def heads(where, gain, arrays, normed):
    rows, width = arrays[0].shape
    out = ((len(arrays), rows, width // 2), LOW)
    return call(functools.partial(heads_body, normed), [out, out], 1, where, gain, *arrays)


def pick_back_body(where_ref, plan_ref, *refs):
    *around, out = refs
    column = where_ref[0] % 4
    for tick in range(MICRO):
        distance = (plan_at(plan_ref, 0, tick, column, 0) - column + 4) % 4
        for k in range(4):

            @pl.when(distance == k)
            def _(k=k, tick=tick):
                out[tick] = around[k][tick]


def pick_out_body(where_ref, plan_ref, *refs):
    *around, out = refs
    column = where_ref[0] % 4
    out[...] = jnp.zeros_like(out)
    for tick in range(MICRO):
        for k in range(4):
            heading = plan_at(plan_ref, 1, tick, (column + k) % 4, 0) == column

            @pl.when(heading & (where_ref[0] >= 4))
            def _(k=k, tick=tick):
                out[tick] = around[k][tick]


def columns_of(plan_ref, which, tick, row, e, width):
    start = plan_at(plan_ref, which, tick, row, 1 + e) * width
    return pl.ds(pl.multiple_of(start, width), width)


def stash_body(where_ref, plan_ref, gain_ref, own, fetched, old, keep_ref, send_ref):
    width = fetched.shape[-1]
    row = jnp.minimum(where_ref[0], 3)
    for tick in range(MICRO):
        old[tick] = own[tick]

        @pl.when(where_ref[0] < 4)
        def _(tick=tick):
            for e in range(EVICT):
                old[tick, :, columns_of(plan_ref, 0, tick, row, e, width)] = fetched[tick, e]

        store_split(where_ref, tick, norm_of(old[tick], gain_ref[...]), keep_ref, send_ref)


def leave_body(where_ref, plan_ref, first, second, pulled, kept):
    width = pulled.shape[-1]
    row = jnp.minimum(where_ref[0], 3)
    for tick, x in enumerate((first, second)):
        kept[tick] = x[...]
        for e in range(EVICT):
            columns = columns_of(plan_ref, 1, tick, row, e, width)
            pulled[tick, e] = x[:, columns]

            @pl.when(where_ref[0] < 4)
            def _(tick=tick, columns=columns):
                kept[tick, :, columns] = jnp.zeros((kept.shape[1], width), kept.dtype)


def sides(where_ref, keep, got):
    low_z = where_ref[1] == 0
    a, b = keep[...].astype(WIDE), got[...].astype(WIDE)
    return jnp.where(low_z, a, b), jnp.where(low_z, b, a)


def add_body(where_ref, values, keep, got, out):
    half = keep.shape[1]
    left, right = sides(where_ref, keep, got)
    out[:, :half] = (values[:, :half].astype(WIDE) + left).astype(LOW)
    out[:, half:] = (values[:, half:].astype(WIDE) + right).astype(LOW)


def finish_body(where_ref, gain_ref, values, cotangent, keep, got, out, part):
    half = keep.shape[1]
    width = 2 * half
    wide = values[...].astype(WIDE)
    inverse_rms = lax.rsqrt(jnp.mean(wide * wide, axis=-1, keepdims=True) + EPSILON)
    cubed = inverse_rms * inverse_rms * inverse_rms
    pieces = []
    for at, d_normed in zip((0, half), sides(where_ref, keep, got)):
        columns = slice(at, at + half)
        v = values[:, columns].astype(WIDE)
        part[:, columns] = jnp.sum(d_normed * v * inverse_rms, axis=0, keepdims=True)
        scaled = d_normed * gain_ref[:, columns]
        pieces.append((columns, v, scaled, jnp.sum(scaled * v, axis=-1, keepdims=True)))
    mean = (pieces[0][3] + pieces[1][3]) / width
    for columns, v, scaled, _ in pieces:
        g = cotangent[:, columns].astype(WIDE)
        out[:, columns] = (g + inverse_rms * scaled - v * cubed * mean).astype(LOW)


def ordered(at_zero, own, other):
    return jnp.where(at_zero, own, other), jnp.where(at_zero, other, own)


class Gather:
    def __init__(self, order, low_z, keep, send):
        self.order, self.low_z, self.keep, self.outgoing = order, low_z, keep, send

    def z(self):
        self.got = self.order.send_z(self.outgoing)

    def y(self):
        self.got = self.order.take_z(self.got)
        self.mine = jnp.stack(ordered(self.low_z, self.keep, self.got))
        self.before, self.behind = self.order.send_both_ways(self.mine, self.mine)

    def far(self):
        self.before, self.behind = self.order.take(self.before, self.behind)
        both = self.order.send_both_ways(self.before[0], self.behind[1])
        self.far_low, self.far_high = both

    def core(self):
        self.far_low, self.far_high = self.order.take(self.far_low, self.far_high)
        self.ring = [
            jnp.stack(
                [
                    self.mine[:, k],
                    self.behind[:, k],
                    jnp.stack([self.far_low[k], self.far_high[k]]),
                    self.before[:, k],
                ]
            )
            for k in range(self.keep.shape[0])
        ]
        self.swapped = [self.order.send(r, TO_CORE) for r in self.ring]

    def rows(self):
        half = self.keep.shape[-1]
        self.swapped = self.order.take(*self.swapped)
        return [
            jnp.concatenate([r, s]).reshape(-1, half) for r, s in zip(self.ring, self.swapped)
        ]


class Settle:
    def __init__(self, order, low_z):
        self.order, self.low_z = order, low_z

    def core(self, part):
        half = part.shape[0] // 2
        self.kept = part[:half]
        self.got = self.order.send(part[half:].astype(LOW), TO_CORE)

    def far(self):
        half, width = self.kept.shape
        (self.got,) = self.order.take(self.got)
        self.summed = (self.kept + self.got.astype(WIDE)).reshape(4, 2, half // 8, width)
        far = self.summed[2].astype(LOW)
        self.low, self.high = self.order.send_both_ways(far[0], far[1])

    def y(self):
        s = self.summed
        self.low, self.high = self.order.take(self.low, self.high)
        up = jnp.stack([s[1, 0] + self.low.astype(WIDE), s[1, 1]]).astype(LOW)
        down = jnp.stack([s[3, 0], s[3, 1] + self.high.astype(WIDE)]).astype(LOW)
        self.first, self.second = self.order.send_both_ways(up, down)

    def z(self):
        self.first, self.second = self.order.take(self.first, self.second)
        mine = self.summed[0] + self.first.astype(WIDE) + self.second.astype(WIDE)
        mine = mine.astype(LOW)
        self.keep = jnp.where(self.low_z, mine[0], mine[1])
        self.got = self.order.send_z(jnp.where(self.low_z, mine[1], mine[0]))

    def end(self):
        self.got = self.order.take_z(self.got)
        return self.keep, self.got


class Bulk:
    def __init__(self, order, part, chunks):
        self.order, self.own = order, part.astype(LOW)
        self.size = part.shape[0] // chunks
        self.landed, self.taken = [], 0
        order.bulks.append(self)

    def z(self):
        at = len(self.landed) * self.size
        self.landed.append(self.order.send(self.own[at : at + self.size], TO_Z))

    def take(self):
        i = self.taken
        self.landed[i] = self.order.tie(self.landed[i])
        self.taken = i + 1

    def total(self):
        self.landed = list(self.order.take(*self.landed))
        self.taken = len(self.landed)
        got = self.landed[0] if len(self.landed) == 1 else jnp.concatenate(self.landed)
        return self.own.astype(WIDE) + got.astype(WIDE)


def times(a, b):
    return jnp.dot(a, b, preferred_element_type=WIDE)


def times_transposed(a, b):
    return lax.dot_general(a, b, (((1,), (1,)), ((), ())), preferred_element_type=WIDE)


def over_rows(a, b):
    return lax.dot_general(a, b, (((0,), (0,)), ((), ())), preferred_element_type=WIDE)


def activations(hidden_pre, d_hidden):
    gate = jax.nn.sigmoid(hidden_pre)
    hidden = (hidden_pre * gate).astype(LOW)
    return hidden, (d_hidden * gate * (1.0 + hidden_pre * (1.0 - gate))).astype(LOW)


def local(
    act_in, act_first, grad_in, grad_last, stash_local, stash_guest, plan, norm_gain, w_up, w_down
):
    order = Order()
    section, d = lax.axis_index("pipe"), lax.axis_index("dp")
    z, core = d // 2, d % 2
    low_z, low_core = z == 0, core == 0
    where = jnp.stack([section, z]).astype(jnp.int32)
    plan = plan.reshape(-1)
    rows, width = act_in.shape[1:]
    whole = ((rows, width), LOW)
    parcel = (stash_guest.shape[1:], LOW)

    def gather(keep, send):
        return Gather(order, low_z, keep, send)

    def swap_hidden(*owns):
        return [(own, order.send(own, TO_CORE)) for own in owns]

    def whole_hidden(*pairs):
        wholes = []
        for own, got in pairs:
            (got,) = order.take(got)
            half = own.shape[0] // 2
            other = jnp.concatenate([got[half:], got[:half]])
            wholes.append(order.done(jnp.concatenate(ordered(low_core, own, other), axis=1)))
        return wholes

    def my_features(x):
        half = x.shape[1] // 2
        return jnp.where(low_core, x[:, :half], x[:, half:])

    def finished(values, cotangent, settled):
        outs = [whole, ((1, width), WIDE)]
        args = (where, norm_gain, values, cotangent, *settled.end())
        return call(finish_body, outs, 1, *args)

    first = gather(*heads(where, norm_gain, [grad_in[0], act_in[0]], (False, True)))
    first.z()
    held = stash_guest[0]
    around = [held] + [order.send(held, round_x(step)) for step in (-1, -2, 1)]

    (found,) = call(pick_back_body, [parcel], 2, where, plan, *order.take(*around))
    guests = order.send(found, TO_EARLY)
    first.y()
    w_up, w_down = order.take(w_up, w_down)
    half = w_up.shape[2] // 2
    here, there = core * half, (1 - core) * half
    down_got = order.send(lax.dynamic_slice_in_dim(w_down[0], there, half, 0), TO_CORE)
    up_got = order.send(lax.dynamic_slice_in_dim(w_up[0], there, half, 1), TO_CORE)
    (down_got,) = order.take(down_got)
    down_own = lax.dynamic_slice_in_dim(w_down[0], here, half, 0)
    down = order.done(jnp.concatenate(ordered(low_core, down_own, down_got), axis=1))
    first.far()
    (up_got,) = order.take(up_got)
    up_own = lax.dynamic_slice_in_dim(w_up[0], here, half, 1)
    up = order.done(jnp.concatenate(ordered(low_core, up_own, up_got), axis=0))

    pair = ((MICRO, rows, width // 2), LOW)
    old, *split = call(
        stash_body,
        [((MICRO, rows, width), LOW), pair, pair],
        2,
        where,
        plan,
        norm_gain,
        stash_local[0],
        *order.take(guests),
    )
    stash = gather(*split)
    stash.z()
    first.core()
    cot_rows_zero, front_rows_zero = first.rows()
    stash.y()
    d_hidden_zero = Bulk(order, times_transposed(cot_rows_zero, down), 1)
    d_hidden_zero.z()
    stash.far()
    stash.core()
    stash_rows = stash.rows()
    pre_zero = Bulk(order, times(stash_rows[0], up), 1)
    pre_zero.z()
    front_pre_zero = Bulk(order, times(front_rows_zero, up), 4)
    front_pre_zero.z()
    pre_one = Bulk(order, order.done(times(stash_rows[1], up).astype(LOW)), 2)

    hidden_zero, d_pre_zero = activations(pre_zero.total(), d_hidden_zero.total())
    back = Settle(order, low_z)
    d_rows = order.done(times_transposed(d_pre_zero, up))
    front_pre_zero.z()
    front_pre_zero.take()
    back.core(d_rows)
    front_pre_zero.z()
    front_pre_zero.take()
    back.far()
    front_pre_zero.z()
    front_pre_zero.take()
    back.y()
    back.z()
    hidden_zero, d_pre_zero = swap_hidden(hidden_zero, d_pre_zero)
    d_input_zero, gain_zero = finished(old[0], grad_in[0], back)
    returned = order.send(d_input_zero, LAST)

    front = Settle(order, low_z)
    front_hidden = jax.nn.silu(front_pre_zero.total()).astype(LOW)
    front.core(times(front_hidden, down))
    cot_one = jnp.where(section == 7, grad_last, order.take(returned)[0])
    second = gather(*heads(where, norm_gain, [cot_one], (False,)))
    second.z()
    pre_one.z()
    pre_one.z()
    front.far()
    second.y()
    front.y()
    second.far()
    front.z()
    second.core()
    (cot_rows_one,) = second.rows()
    d_hidden_one = Bulk(order, times_transposed(cot_rows_one, down), 2)
    d_hidden_one.z()
    (front_zero,) = call(add_body, [whole], 1, where, act_in[0], *front.end())
    passed = order.send(front_zero, NEXT)
    hidden_zero, d_pre_zero = whole_hidden(hidden_zero, d_pre_zero)
    grad_up = order.done(over_rows(my_features(stash_rows[0]), d_pre_zero))
    input_one = jnp.where(section == 0, act_first, order.take(passed)[0])
    third = gather(*heads(where, norm_gain, [input_one], (True,)))
    third.z()
    d_hidden_one.z()
    pulled, kept = call(
        leave_body,
        [parcel, ((MICRO, rows, width), LOW)],
        2,
        where,
        plan,
        act_in[0],
        input_one,
    )
    landed = order.send(pulled, TO_LATE)
    third.y()
    grad_down = order.done(over_rows(hidden_zero, my_features(cot_rows_zero)))
    third.far()
    landed = order.tie(landed)
    third.core()
    (front_rows_one,) = third.rows()
    part = order.done(times(front_rows_one, up).astype(LOW))
    front_pre_one = Bulk(order, part, 4)
    front_pre_one.z()
    front_pre_one.z()

    hidden_one, d_pre_one = activations(pre_one.total(), d_hidden_one.total())
    back = Settle(order, low_z)
    d_rows = order.done(times_transposed(d_pre_one, up))
    back.core(d_rows)
    hidden_one, d_pre_one = swap_hidden(hidden_one, d_pre_one)
    around = [landed] + [order.send(landed, round_x(step)) for step in (-1, -2, 1)]
    front_pre_one.take()
    front_pre_one.z()
    hidden_one, d_pre_one = whole_hidden(hidden_one, d_pre_one)
    more = over_rows(my_features(stash_rows[1]), d_pre_one)
    grad_up = order.done((grad_up + more).astype(LOW))
    front_pre_one.take()
    front_pre_one.z()
    back.far()
    (guest_new,) = call(pick_out_body, [parcel], 2, where, plan, *order.take(*around))
    guest_new = order.done(guest_new)
    more = over_rows(hidden_one, my_features(cot_rows_one))
    grad_down = order.done((grad_down + more).astype(LOW))
    front_pre_one.take()
    back.y()
    front_pre_one.take()

    front = Settle(order, low_z)
    front_hidden = jax.nn.silu(front_pre_one.total()).astype(LOW)
    front.core(times(front_hidden, down))
    back.z()
    d_input_one, gain_one = finished(old[1], cot_one, back)
    gain = gain_zero + gain_one
    gain = gain + order.send(gain, TO_CORE)
    front.far()
    gain = gain + order.send(gain, TO_Z)
    front.y()
    front.z()
    gain = gain + order.send(gain, ("tensor", [(t, t ^ 1) for t in range(4)]))
    gain = gain + order.send(gain, ("tensor", [(t, t ^ 2) for t in range(4)]))
    (front_one,) = call(add_body, [whole], 1, where, input_one, *front.end())

    return (
        jnp.stack([front_zero, front_one])[None],
        jnp.stack([d_input_zero, d_input_one])[None],
        kept[None],
        guest_new[None],
        grad_up[None],
        grad_down[None],
        gain,
    )


def solution(mesh):
    placed = (
        P("pipe", ("dp", "tensor"), None),
        P(("dp", "tensor"), None),
        P("pipe", ("dp", "tensor"), None),
        P(("dp", "tensor"), None),
        P("pipe", None, ("dp", "tensor"), None),
        P("pipe", None, None, ("dp", "tensor"), None),
        P(),
        P("pipe", None),
        P("pipe", "dp", "tensor"),
        P("pipe", "tensor", "dp"),
    )
    return jax.shard_map(
        local,
        mesh=mesh,
        in_specs=placed,
        out_specs=(
            P("pipe", None, ("dp", "tensor"), None),
            P("pipe", None, ("dp", "tensor"), None),
            P("pipe", None, ("dp", "tensor"), None),
            P("pipe", None, None, ("dp", "tensor"), None),
            P("pipe", "dp", "tensor"),
            P("pipe", "tensor", "dp"),
            P("pipe", None),
        ),
        check_vma=False,
    )
```
